32 devices in a mesh: gy: 8 (over y, x, core), gx: 4 (over z).
Axes of the slice: x: 2, y: 2, z: 4, core: 2. Of those that a mesh axis runs over, the one named last changes fastest.
Arguments:
- inputs: bfloat16 [1, 512, 256, 384], P(None, 'gy', 'gx'), may hold values from -6 to 6
- nearby_kernel: bfloat16 [3, 3, 384, 384], replicated, may hold values from -0.109375 to 0.109375
- nearby_bias: float32 [384], replicated, may hold values from -3 to 3
- distant_kernel: bfloat16 [3, 3, 384, 384], replicated, may hold values from -0.109375 to 0.109375
- distant_bias: float32 [384], replicated, may hold values from -3 to 3
Outputs:
- outputs: bfloat16 [1, 512, 256, 384], P(None, 'gy', 'gx')
The draws below stay inside these ranges and needn't reach their ends.
All inputs are finite; a program needn't handle non-finite values.
Results may differ from the reference program's by a relative error of at most 0.004.
Values may be sent and summed in bfloat16 or wider, within the bound.
A program may use at most 128 MiB of HBM per device.

```python
import jax
import jax.numpy as jnp
from jax import lax

C = 384
NEAR_DILATION = 4
FAR_DILATION = 64
BATCH = 1
H = 512
W = 256


def block_levels(stream_key, shape, shards, low, high):
    gain = 1.0
    for dim, shards_of in shards:
        steps = jax.random.uniform(jax.random.fold_in(jax.random.fold_in(stream_key, 6), dim), (shards_of,), jnp.float32, low / len(shards), high / len(shards))
        gain = gain * jnp.repeat(jnp.exp(steps), shape[dim] // shards_of).reshape((-1,) + (1,) * (len(shape) - 1 - dim))
    return gain


def centred(own_key, shape, deviation, bound, pieces=(), kind=jnp.bfloat16):
    factor_of = block_levels(own_key, shape, pieces, -0.22, 0.18) if pieces else 1.0
    values = jax.random.normal(own_key, shape, jnp.float32) * deviation * factor_of
    return jnp.minimum(jnp.maximum(values, -bound), bound).astype(kind)


def setup_inputs(seed: int = 0) -> dict:
    key_list = jax.random.split(jax.random.key(seed), 6)
    return {
        "inputs": centred(key_list[0], (BATCH, H, W, C), 1.0, 6.0, ((1, 8), (2, 4))),
        "nearby_kernel": centred(key_list[1], (3, 3, C, C), (9 * C) ** -0.5, 0.109375),
        "nearby_bias": centred(key_list[2], (C,), 0.5, 3.0, (), jnp.float32),
        "distant_kernel": centred(key_list[3], (3, 3, C, C), (9 * C) ** -0.5, 0.109375),
        "distant_bias": centred(key_list[4], (C,), 0.5, 3.0, (), jnp.float32),
    }


def apply_convolution(input_field, kernel_weight, dilation_rate):
    return lax.conv_general_dilated(input_field.astype(jnp.float32), kernel_weight.astype(jnp.float32), (1, 1), ((dilation_rate, dilation_rate), (dilation_rate, dilation_rate)), rhs_dilation=(dilation_rate, dilation_rate), dimension_numbers=("NHWC", "HWIO", "NHWC"), precision=lax.Precision.HIGHEST)


def reference(inputs, nearby_kernel, nearby_bias, distant_kernel, distant_bias):
    hidden_state = jax.nn.gelu(apply_convolution(inputs, nearby_kernel, NEAR_DILATION) + nearby_bias, approximate=False).astype(jnp.bfloat16)
    branch_output = jax.nn.gelu(apply_convolution(hidden_state, distant_kernel, FAR_DILATION) + distant_bias, approximate=False).astype(jnp.bfloat16)
    return (inputs.astype(jnp.float32) + branch_output.astype(jnp.float32)).astype(jnp.bfloat16)
```

```python
import functools

import jax
import jax.numpy as jnp
from jax import lax
from jax.experimental import pallas as pl
from jax.experimental.pallas import tpu as pltpu
from jax.sharding import PartitionSpec as P

MESH = pl.DeviceIdType.MESH
D = 4
DIRS = [(-1, 0), (1, 0), (0, -1), (0, 1), (-1, -1), (-1, 1), (1, -1), (1, 1)]


def gelu(v):
    return v * (1.0 + lax.erf(v * 0.7071067811865476)) * 0.5


def body(ny, nx, x_ref, w1_ref, b1_ref, w2_ref, b2_ref, o_ref,
         xp, w1, w2, h, hl, hr, su, sd, ru, rd, own, ob,
         halo_s, halo_r, loc, hs, hrv, ps, prv, osem):
    gy = lax.axis_index("gy")
    gx = lax.axis_index("gx")
    n, m, c = h.shape
    g = n

    def there(dy, dx):
        ok = None
        for idx, d, size in ((gy, dy, ny), (gx, dx, nx)):
            if d:
                t = idx > 0 if d < 0 else idx < size - 1
                ok = t if ok is None else jnp.logical_and(ok, t)
        return ok

    def dev(dy, dx):
        return (lax.rem(gy + dy + ny, ny), lax.rem(gx + dx + nx, nx))

    load_x = pltpu.make_async_copy(x_ref, xp.at[pl.ds(1, g), pl.ds(1, g)], loc.at[0])
    load_w1 = pltpu.make_async_copy(w1_ref, w1, loc.at[1])
    load_w2 = pltpu.make_async_copy(w2_ref, w2, loc.at[2])
    load_x.start()
    load_w1.start()
    load_w2.start()

    edge = jnp.zeros((g + 2, 16, c), xp.dtype)
    xp[0] = edge
    xp[g + 1] = edge
    xp[pl.ds(1, g), 0] = edge[:g]
    xp[pl.ds(1, g), g + 1] = edge[:g]

    barrier = pltpu.get_barrier_semaphore()
    for d in DIRS:
        @pl.when(there(*d))
        def _(d=d):
            pl.semaphore_signal(barrier, inc=1, device_id=dev(*d), device_id_type=MESH)
    pl.semaphore_wait(barrier, sum(there(*d).astype(jnp.int32) for d in DIRS))

    def halo(i):
        dy, dx = DIRS[i]
        src = [0 if s < 0 else g - 1 if s > 0 else None for s in (dy, dx)]
        src = tuple(pl.ds(0, g) if s is None else pl.ds(s, 1) for s in src)
        dst = [g + 1 if s < 0 else 0 if s > 0 else None for s in (dy, dx)]
        dst = tuple(pl.ds(1, g) if s is None else pl.ds(s, 1) for s in dst)
        return pltpu.make_async_remote_copy(
            src_ref=x_ref.at[src], dst_ref=xp.at[dst], send_sem=halo_s.at[i],
            recv_sem=halo_r.at[i], device_id=dev(dy, dx), device_id_type=MESH)

    for i, d in enumerate(DIRS):
        @pl.when(there(*d))
        def _(i=i):
            halo(i).start()

    for buf, d in ((hl, (0, -1)), (hr, (0, 1)), (ru, (-1, 0)), (rd, (1, 0))):
        @pl.when(jnp.logical_not(there(*d)))
        def _(buf=buf):
            def zero(k, carry):
                buf[k] = jnp.zeros((m, c), buf.dtype)
                return carry
            lax.fori_loop(0, n, zero, 0)

    load_x.wait()
    load_w1.wait()
    for i, d in enumerate(DIRS):
        @pl.when(there(-d[0], -d[1]))
        def _(i=i):
            halo(i).wait_recv()

    def send_h(k, right):
        return pltpu.make_async_remote_copy(
            src_ref=h.at[k], dst_ref=(hl if right else hr).at[k],
            send_sem=hs.at[int(right), k], recv_sem=hrv.at[int(right), k],
            device_id=dev(0, 1 if right else -1), device_id_type=MESH)

    def send_p(k, down):
        return pltpu.make_async_remote_copy(
            src_ref=(sd if down else su).at[k], dst_ref=(ru if down else rd).at[k],
            send_sem=ps.at[int(down), k], recv_sem=prv.at[int(down), k],
            device_id=dev(1 if down else -1, 0), device_id_type=MESH)

    has_l, has_r, has_u, has_d = there(0, -1), there(0, 1), there(-1, 0), there(1, 0)

    def near(k, carry):
        acc = None
        for a in range(3):
            for e in range(3):
                lhs = xp[k + a, pl.ds(e, g)].reshape(m, c)
                t = jnp.dot(lhs, w1[a * 3 + e], preferred_element_type=jnp.float32)
                acc = t if acc is None else acc + t
        h[k] = gelu(acc + b1_ref[...]).astype(h.dtype)

        @pl.when(has_r)
        def _():
            send_h(k, True).start()

        @pl.when(has_l)
        def _():
            send_h(k, False).start()
        return carry

    lax.fori_loop(0, n, near, 0)
    load_w2.wait()

    def finish(k):
        @pl.when(has_u)
        def _():
            send_p(k, True).wait_recv()

        @pl.when(has_d)
        def _():
            send_p(k, False).wait_recv()
        v = own[k] + ru[k].astype(jnp.float32) + rd[k].astype(jnp.float32) + b2_ref[...]
        branch = gelu(v).astype(jnp.bfloat16).astype(jnp.float32)
        x = xp[k + 1, pl.ds(1, g)].reshape(m, c).astype(jnp.float32)
        ob[k] = (x + branch).astype(ob.dtype)
        pltpu.make_async_copy(ob.at[k], o_ref.at[k], osem.at[k]).start()

    def far_sum(k, a):
        acc = None
        for e, v in enumerate((hl, h, hr)):
            t = jnp.dot(v[k], w2[a * 3 + e], preferred_element_type=jnp.float32)
            acc = t if acc is None else acc + t
        return acc

    def far(k, carry):
        @pl.when(has_l)
        def _():
            send_h(k, True).wait_recv()

        @pl.when(has_r)
        def _():
            send_h(k, False).wait_recv()
        sd[k] = far_sum(k, 0).astype(sd.dtype)
        su[k] = far_sum(k, 2).astype(su.dtype)

        @pl.when(has_d)
        def _():
            send_p(k, True).start()

        @pl.when(has_u)
        def _():
            send_p(k, False).start()
        own[k] = far_sum(k, 1)

        @pl.when(k > 0)
        def _():
            finish(k - 1)
        return carry

    lax.fori_loop(0, n, far, 0)
    finish(n - 1)

    for i, d in enumerate(DIRS):
        @pl.when(there(*d))
        def _(i=i):
            halo(i).wait_send()

    def drain(k, carry):
        for ok, make, flag in ((has_r, send_h, True), (has_l, send_h, False),
                               (has_d, send_p, True), (has_u, send_p, False)):
            @pl.when(ok)
            def _(make=make, flag=flag):
                make(k, flag).wait_send()
        pltpu.make_async_copy(ob.at[k], o_ref.at[k], osem.at[k]).wait()
        return carry

    lax.fori_loop(0, n, drain, 0)


def on_device(inputs, nearby_kernel, nearby_bias, distant_kernel, distant_bias):
    _, rows, cols, c = inputs.shape
    ny, nx = lax.axis_size("gy"), lax.axis_size("gx")
    g = rows // D
    m = cols * D
    blocks = inputs.reshape(g, D, cols // D, D, c).transpose(0, 2, 1, 3, 4).reshape(g, g, D * D, c)
    bf, f32 = jnp.bfloat16, jnp.float32
    tile = pltpu.VMEM((g, m, c), bf)
    dma = pltpu.SemaphoreType.DMA
    hbm = pl.BlockSpec(memory_space=pl.ANY)
    vmem = pl.BlockSpec(memory_space=pltpu.VMEM)
    out = pl.pallas_call(
        functools.partial(body, ny, nx),
        out_shape=jax.ShapeDtypeStruct((g, m, c), bf),
        in_specs=[hbm, hbm, vmem, hbm, vmem],
        out_specs=hbm,
        scratch_shapes=[
            pltpu.VMEM((g + 2, g + 2, D * D, c), bf),
            pltpu.VMEM((9, c, c), bf),
            pltpu.VMEM((9, c, c), bf),
            tile, tile, tile, tile, tile, tile, tile,
            pltpu.VMEM((g, m, c), f32),
            tile,
            dma((8,)), dma((8,)), dma((3,)),
            dma((2, g)), dma((2, g)), dma((2, g)), dma((2, g)), dma((g,)),
        ],
        compiler_params=pltpu.CompilerParams(
            collective_id=0, has_side_effects=True, vmem_limit_bytes=56 * 1024 * 1024),
        cost_estimate=pl.CostEstimate(
            flops=36 * rows * cols * c * c, bytes_accessed=16 * 2**20, transcendentals=0),
    )(blocks, nearby_kernel.reshape(9, c, c), nearby_bias.reshape(1, c),
      distant_kernel.reshape(9, c, c), distant_bias.reshape(1, c))
    return out.reshape(g, g, D, D, c).transpose(0, 2, 1, 3, 4).reshape(1, rows, cols, c)


def solution(mesh):
    placed = (P(None, "gy", "gx", None), P(), P(), P(), P())
    return jax.shard_map(
        on_device, mesh=mesh, in_specs=placed, out_specs=P(None, "gy", "gx", None), check_vma=False
    )
```

```python
import functools

import jax
import jax.numpy as jnp
from jax import lax
from jax.experimental import pallas as pl
from jax.experimental.pallas import tpu as pltpu
from jax.sharding import PartitionSpec as P

MESH = pl.DeviceIdType.MESH
D = 4
LAG = 4
LATE = 2
DIRS = [(-1, 0), (1, 0), (0, -1), (0, 1), (-1, -1), (-1, 1), (1, -1), (1, 1)]


def swap(a, b):
    n, c = a.size // (8 * a.shape[-1]), a.shape[-1]
    low = lax.broadcasted_iota(jnp.int32, (n, 8, c), 1) < 4
    p, q = a.reshape(n, 8, c), b.reshape(n, 8, c)
    first = jnp.where(low, p, pltpu.roll(q, 4, 1))
    second = jnp.where(low, pltpu.roll(p, 4, 1), q)
    return first.reshape(a.shape), second.reshape(a.shape)


def to_blocks(v):
    c = v.shape[-1]
    t = v.shape[1] // 16
    v = v.reshape(2, 2, t, 2, 8, c)
    parts = [swap(v[i, 0], v[i, 1]) for i in range(2)]
    out = jnp.stack([jnp.stack([parts[i][hi] for i in range(2)], axis=2) for hi in range(2)], axis=2)
    return out.reshape(4 * t, 16, c)


def from_blocks(v):
    c = v.shape[-1]
    t = v.shape[0] // 4
    v = v.reshape(t, 2, 2, 2, 8, c)
    parts = [swap(v[:, :, 0, i], v[:, :, 1, i]) for i in range(2)]
    return jnp.stack([parts[i][odd] for i in range(2) for odd in range(2)], axis=0).reshape(4, 16 * t, c)


def gelu(v):
    return v * (1.0 + lax.erf(v * 0.7071067811865476)) * 0.5


def body(ny, nx, x_ref, w1_ref, b1_ref, w2_ref, b2_ref, o_ref,
         xin, xp, w1, w2, h, hl, hr, su, sd, ru, rd, own, ob,
         halo_s, halo_r, loc, hs, hrv, ps, prv, osem):
    gy = lax.axis_index("gy")
    gx = lax.axis_index("gx")
    n, m, c = h.shape
    g = n

    def there(dy, dx):
        ok = None
        for idx, d, size in ((gy, dy, ny), (gx, dx, nx)):
            if d:
                t = idx > 0 if d < 0 else idx < size - 1
                ok = t if ok is None else jnp.logical_and(ok, t)
        return ok

    def dev(dy, dx):
        return (lax.rem(gy + dy + ny, ny), lax.rem(gx + dx + nx, nx))

    load_x = pltpu.make_async_copy(x_ref, xin, loc.at[0])
    load_w1 = pltpu.make_async_copy(w1_ref, w1, loc.at[1])
    load_w2 = pltpu.make_async_copy(w2_ref, w2, loc.at[2])
    load_x.start()
    load_w1.start()
    load_w2.start()

    edge = jnp.zeros((g + 2, 16, c), xp.dtype)
    xp[0] = edge
    xp[g + 1] = edge
    xp[pl.ds(1, g), 0] = edge[:g]
    xp[pl.ds(1, g), g + 1] = edge[:g]

    barrier = pltpu.get_barrier_semaphore()
    for d in DIRS:
        @pl.when(there(*d))
        def _(d=d):
            pl.semaphore_signal(barrier, inc=1, device_id=dev(*d), device_id_type=MESH)
    load_x.wait()

    def reorder(k, carry):
        xp[k + 1, pl.ds(1, g)] = to_blocks(xin[pl.ds(D * k, D)].astype(jnp.float32)).astype(xp.dtype)
        return carry

    lax.fori_loop(0, g, reorder, 0)
    pl.semaphore_wait(barrier, sum(there(*d).astype(jnp.int32) for d in DIRS))

    def halo(i):
        dy, dx = DIRS[i]
        src = [1 if s < 0 else g if s > 0 else None for s in (dy, dx)]
        src = tuple(pl.ds(1, g) if s is None else pl.ds(s, 1) for s in src)
        dst = [g + 1 if s < 0 else 0 if s > 0 else None for s in (dy, dx)]
        dst = tuple(pl.ds(1, g) if s is None else pl.ds(s, 1) for s in dst)
        return pltpu.make_async_remote_copy(
            src_ref=xp.at[src], dst_ref=xp.at[dst], send_sem=halo_s.at[i],
            recv_sem=halo_r.at[i], device_id=dev(dy, dx), device_id_type=MESH)

    for i, d in enumerate(DIRS):
        @pl.when(there(*d))
        def _(i=i):
            halo(i).start()

    for buf, d in ((hl, (0, -1)), (hr, (0, 1)), (ru, (-1, 0)), (rd, (1, 0))):
        @pl.when(jnp.logical_not(there(*d)))
        def _(buf=buf):
            def zero(k, carry):
                buf[k] = jnp.zeros((m, c), buf.dtype)
                return carry
            lax.fori_loop(0, n, zero, 0)

    load_w1.wait()
    for i, d in enumerate(DIRS):
        @pl.when(there(-d[0], -d[1]))
        def _(i=i):
            halo(i).wait_recv()

    def send_h(k, right):
        return pltpu.make_async_remote_copy(
            src_ref=h.at[k], dst_ref=(hl if right else hr).at[k],
            send_sem=hs.at[int(right), k], recv_sem=hrv.at[int(right), k],
            device_id=dev(0, 1 if right else -1), device_id_type=MESH)

    def send_p(k, down):
        return pltpu.make_async_remote_copy(
            src_ref=(sd if down else su).at[k], dst_ref=(ru if down else rd).at[k],
            send_sem=ps.at[int(down), k], recv_sem=prv.at[int(down), k],
            device_id=dev(1 if down else -1, 0), device_id_type=MESH)

    has_l, has_r, has_u, has_d = there(0, -1), there(0, 1), there(-1, 0), there(1, 0)

    def near(k):
        acc = None
        for a in range(3):
            for e in range(3):
                lhs = xp[k + a, pl.ds(e, g)].reshape(m, c)
                t = jnp.dot(lhs, w1[a * 3 + e], preferred_element_type=jnp.float32)
                acc = t if acc is None else acc + t
        h[k] = gelu(acc + b1_ref[...].reshape(1, c)).astype(h.dtype)

        @pl.when(has_r)
        def _():
            send_h(k, True).start()

        @pl.when(has_l)
        def _():
            send_h(k, False).start()

    def store(k):
        rows = pl.ds(D * k, D)
        return pltpu.make_async_copy(ob.at[rows], o_ref.at[rows], osem.at[k])

    def finish(k):
        @pl.when(has_u)
        def _():
            send_p(k, True).wait_recv()

        @pl.when(has_d)
        def _():
            send_p(k, False).wait_recv()
        v = own[k] + ru[k].astype(jnp.float32) + rd[k].astype(jnp.float32) + b2_ref[...].reshape(1, c)
        branch = gelu(v).astype(jnp.bfloat16).astype(jnp.float32)
        x = xp[k + 1, pl.ds(1, g)].reshape(m, c).astype(jnp.float32)
        ob[pl.ds(D * k, D)] = from_blocks((x + branch).reshape(g, 16, c)).astype(ob.dtype)
        store(k).start()

    def far_sum(k, a):
        acc = None
        for e, v in enumerate((hl, h, hr)):
            t = jnp.dot(v[k], w2[a * 3 + e], preferred_element_type=jnp.float32)
            acc = t if acc is None else acc + t
        return acc

    def far(k):
        @pl.when(has_l)
        def _():
            send_h(k, True).wait_recv()

        @pl.when(has_r)
        def _():
            send_h(k, False).wait_recv()
        sd[k] = far_sum(k, 0).astype(sd.dtype)
        su[k] = far_sum(k, 2).astype(su.dtype)

        @pl.when(has_d)
        def _():
            send_p(k, True).start()

        @pl.when(has_u)
        def _():
            send_p(k, False).start()
        own[k] = far_sum(k, 1)

    def ahead(k, carry):
        near(k)
        return carry

    def both(k, carry):
        near(k + LAG)
        far(k)

        @pl.when(k >= LATE)
        def _():
            finish(k - LATE)
        return carry

    def behind(k, carry):
        far(k)
        finish(k - LATE)
        return carry

    def last(k, carry):
        finish(k)
        return carry

    lax.fori_loop(0, LAG, ahead, 0)
    load_w2.wait()
    lax.fori_loop(0, n - LAG, both, 0)
    lax.fori_loop(n - LAG, n, behind, 0)
    lax.fori_loop(n - LATE, n, last, 0)

    for i, d in enumerate(DIRS):
        @pl.when(there(*d))
        def _(i=i):
            halo(i).wait_send()

    def drain(k, carry):
        for ok, make, flag in ((has_r, send_h, True), (has_l, send_h, False),
                               (has_d, send_p, True), (has_u, send_p, False)):
            @pl.when(ok)
            def _(make=make, flag=flag):
                make(k, flag).wait_send()
        store(k).wait()
        return carry

    lax.fori_loop(0, n, drain, 0)


def on_device(inputs, nearby_kernel, nearby_bias, distant_kernel, distant_bias):
    _, rows, cols, c = inputs.shape
    ny, nx = lax.axis_size("gy"), lax.axis_size("gx")
    g = rows // D
    m = cols * D
    bf, f32 = jnp.bfloat16, jnp.float32
    tile = pltpu.VMEM((g, m, c), bf)
    dma = pltpu.SemaphoreType.DMA
    hbm = pl.BlockSpec(memory_space=pl.ANY)
    vmem = pl.BlockSpec(memory_space=pltpu.VMEM)
    out = pl.pallas_call(
        functools.partial(body, ny, nx),
        out_shape=jax.ShapeDtypeStruct((rows, cols, c), bf),
        in_specs=[hbm, hbm, vmem, hbm, vmem],
        out_specs=hbm,
        scratch_shapes=[
            pltpu.VMEM((rows, cols, c), bf),
            pltpu.VMEM((g + 2, g + 2, D * D, c), bf),
            pltpu.VMEM((9, c, c), bf),
            pltpu.VMEM((9, c, c), bf),
            tile, tile, tile, tile, tile, tile, tile,
            pltpu.VMEM((g, m, c), f32),
            pltpu.VMEM((rows, cols, c), bf),
            dma((8,)), dma((8,)), dma((3,)),
            dma((2, g)), dma((2, g)), dma((2, g)), dma((2, g)), dma((g,)),
        ],
        compiler_params=pltpu.CompilerParams(
            collective_id=0, has_side_effects=True, vmem_limit_bytes=56 * 1024 * 1024),
        cost_estimate=pl.CostEstimate(
            flops=36 * rows * cols * c * c, bytes_accessed=16 * 2**20, transcendentals=0),
    )(inputs.reshape(rows, cols, c), nearby_kernel.reshape(9, c, c), nearby_bias,
      distant_kernel.reshape(9, c, c), distant_bias)
    return out.reshape(1, rows, cols, c)


def solution(mesh):
    placed = (P(None, "gy", "gx", None), P(), P(), P(), P())
    return jax.shard_map(
        on_device, mesh=mesh, in_specs=placed, out_specs=P(None, "gy", "gx", None), check_vma=False
    )
```

```python
import functools

import jax
import jax.numpy as jnp
from jax import lax
from jax.experimental import pallas as pl
from jax.experimental.pallas import tpu as pltpu
from jax.sharding import PartitionSpec as P

MESH = pl.DeviceIdType.MESH
D = 4
LAG = 3
LATE = 1
DIRS = [(-1, 0), (1, 0), (0, -1), (0, 1), (-1, -1), (-1, 1), (1, -1), (1, 1)]


def swap(a, b):
    n, c = a.size // (8 * a.shape[-1]), a.shape[-1]
    low = lax.broadcasted_iota(jnp.int32, (n, 8, c), 1) < 4
    p, q = a.reshape(n, 8, c), b.reshape(n, 8, c)
    first = jnp.where(low, p, pltpu.roll(q, 4, 1))
    second = jnp.where(low, pltpu.roll(p, 4, 1), q)
    return first.reshape(a.shape), second.reshape(a.shape)


def to_blocks(v):
    c = v.shape[-1]
    t = v.shape[1] // 16
    v = v.reshape(2, 2, t, 2, 8, c)
    parts = [swap(v[i, 0], v[i, 1]) for i in range(2)]
    out = jnp.stack([jnp.stack([parts[i][hi] for i in range(2)], axis=2) for hi in range(2)], axis=2)
    return out.reshape(4 * t, 16, c)


def from_blocks(v):
    c = v.shape[-1]
    t = v.shape[0] // 4
    v = v.reshape(t, 2, 2, 2, 8, c)
    parts = [swap(v[:, :, 0, i], v[:, :, 1, i]) for i in range(2)]
    return jnp.stack([parts[i][odd] for i in range(2) for odd in range(2)], axis=0).reshape(4, 16 * t, c)


def gelu(v):
    return v * (1.0 + lax.erf(v * 0.7071067811865476)) * 0.5


def body(ny, nx, x_ref, w1_ref, b1_ref, w2_ref, b2_ref, o_ref,
         xin, xp, w1, w2, h, hl, hr, su, sd, ru, rd, own, ob,
         halo_s, halo_r, loc, hs, hrv, ps, prv, osem):
    gy = lax.axis_index("gy")
    gx = lax.axis_index("gx")
    n, m, c = h.shape
    g = n

    def there(dy, dx):
        ok = None
        for idx, d, size in ((gy, dy, ny), (gx, dx, nx)):
            if d:
                t = idx > 0 if d < 0 else idx < size - 1
                ok = t if ok is None else jnp.logical_and(ok, t)
        return ok

    def dev(dy, dx):
        return (lax.rem(gy + dy + ny, ny), lax.rem(gx + dx + nx, nx))

    load_x = pltpu.make_async_copy(x_ref, xin, loc.at[0])
    load_w1 = pltpu.make_async_copy(w1_ref, w1, loc.at[1])
    load_w2 = pltpu.make_async_copy(w2_ref, w2, loc.at[2])
    load_x.start()
    load_w1.start()
    load_w2.start()

    edge = jnp.zeros((g + 2, 16, c), xp.dtype)
    xp[0] = edge
    xp[g + 1] = edge
    xp[pl.ds(1, g), 0] = edge[:g]
    xp[pl.ds(1, g), g + 1] = edge[:g]

    barrier = pltpu.get_barrier_semaphore()
    for d in DIRS:
        @pl.when(there(*d))
        def _(d=d):
            pl.semaphore_signal(barrier, inc=1, device_id=dev(*d), device_id_type=MESH)
    load_x.wait()

    def reorder(k, carry):
        xp[k + 1, pl.ds(1, g)] = to_blocks(xin[pl.ds(D * k, D)].astype(jnp.float32)).astype(xp.dtype)
        return carry

    lax.fori_loop(0, g, reorder, 0)
    pl.semaphore_wait(barrier, sum(there(*d).astype(jnp.int32) for d in DIRS))

    def halo(i):
        dy, dx = DIRS[i]
        src = [1 if s < 0 else g if s > 0 else None for s in (dy, dx)]
        src = tuple(pl.ds(1, g) if s is None else pl.ds(s, 1) for s in src)
        dst = [g + 1 if s < 0 else 0 if s > 0 else None for s in (dy, dx)]
        dst = tuple(pl.ds(1, g) if s is None else pl.ds(s, 1) for s in dst)
        return pltpu.make_async_remote_copy(
            src_ref=xp.at[src], dst_ref=xp.at[dst], send_sem=halo_s.at[i],
            recv_sem=halo_r.at[i], device_id=dev(dy, dx), device_id_type=MESH)

    for i, d in enumerate(DIRS):
        @pl.when(there(*d))
        def _(i=i):
            halo(i).start()

    for buf, d in ((hl, (0, -1)), (hr, (0, 1)), (ru, (-1, 0)), (rd, (1, 0))):
        @pl.when(jnp.logical_not(there(*d)))
        def _(buf=buf):
            def zero(k, carry):
                buf[k] = jnp.zeros((m, c), buf.dtype)
                return carry
            lax.fori_loop(0, n, zero, 0)

    load_w1.wait()
    for i, d in enumerate(DIRS):
        @pl.when(there(-d[0], -d[1]))
        def _(i=i):
            halo(i).wait_recv()

    def send_h(k, right):
        return pltpu.make_async_remote_copy(
            src_ref=h.at[k], dst_ref=(hl if right else hr).at[k],
            send_sem=hs.at[int(right), k], recv_sem=hrv.at[int(right), k],
            device_id=dev(0, 1 if right else -1), device_id_type=MESH)

    def send_p(k, down):
        return pltpu.make_async_remote_copy(
            src_ref=(sd if down else su).at[k], dst_ref=(ru if down else rd).at[k],
            send_sem=ps.at[int(down), k], recv_sem=prv.at[int(down), k],
            device_id=dev(1 if down else -1, 0), device_id_type=MESH)

    has_l, has_r, has_u, has_d = there(0, -1), there(0, 1), there(-1, 0), there(1, 0)

    def near(k):
        acc = None
        for a in range(3):
            for e in range(3):
                lhs = xp[k + a, pl.ds(e, g)].reshape(m, c)
                t = jnp.dot(lhs, w1[a * 3 + e], preferred_element_type=jnp.float32)
                acc = t if acc is None else acc + t
        h[k] = gelu(acc + b1_ref[...].reshape(1, c)).astype(h.dtype)

        @pl.when(has_r)
        def _():
            send_h(k, True).start()

        @pl.when(has_l)
        def _():
            send_h(k, False).start()

    def store(k):
        rows = pl.ds(D * k, D)
        return pltpu.make_async_copy(ob.at[rows], o_ref.at[rows], osem.at[k])

    def finish(k):
        @pl.when(has_u)
        def _():
            send_p(k, True).wait_recv()

        @pl.when(has_d)
        def _():
            send_p(k, False).wait_recv()
        v = own[k] + ru[k].astype(jnp.float32) + rd[k].astype(jnp.float32) + b2_ref[...].reshape(1, c)
        branch = gelu(v).astype(jnp.bfloat16).astype(jnp.float32)
        x = xp[k + 1, pl.ds(1, g)].reshape(m, c).astype(jnp.float32)
        ob[pl.ds(D * k, D)] = from_blocks((x + branch).reshape(g, 16, c)).astype(ob.dtype)
        store(k).start()

    def far_sum(k, a):
        acc = None
        for e, v in enumerate((hl, h, hr)):
            t = jnp.dot(v[k], w2[a * 3 + e], preferred_element_type=jnp.float32)
            acc = t if acc is None else acc + t
        return acc

    def far(k):
        @pl.when(has_l)
        def _():
            send_h(k, True).wait_recv()

        @pl.when(has_r)
        def _():
            send_h(k, False).wait_recv()
        sd[k] = far_sum(k, 0).astype(sd.dtype)

        @pl.when(has_d)
        def _():
            send_p(k, True).start()
        su[k] = far_sum(k, 2).astype(su.dtype)

        @pl.when(has_u)
        def _():
            send_p(k, False).start()
        own[k] = far_sum(k, 1)

    def ahead(k, carry):
        near(k)
        return carry

    def both(k, carry):
        near(k + LAG)
        far(k)

        @pl.when(k >= LATE)
        def _():
            finish(k - LATE)
        return carry

    def behind(k, carry):
        far(k)
        finish(k - LATE)
        return carry

    def last(k, carry):
        finish(k)
        return carry

    lax.fori_loop(0, LAG, ahead, 0)
    load_w2.wait()
    lax.fori_loop(0, n - LAG, both, 0)
    lax.fori_loop(n - LAG, n, behind, 0)
    lax.fori_loop(n - LATE, n, last, 0)

    for i, d in enumerate(DIRS):
        @pl.when(there(*d))
        def _(i=i):
            halo(i).wait_send()

    def drain(k, carry):
        for ok, make, flag in ((has_r, send_h, True), (has_l, send_h, False),
                               (has_d, send_p, True), (has_u, send_p, False)):
            @pl.when(ok)
            def _(make=make, flag=flag):
                make(k, flag).wait_send()
        store(k).wait()
        return carry

    lax.fori_loop(0, n, drain, 0)


def on_device(inputs, nearby_kernel, nearby_bias, distant_kernel, distant_bias):
    _, rows, cols, c = inputs.shape
    ny, nx = lax.axis_size("gy"), lax.axis_size("gx")
    g = rows // D
    m = cols * D
    bf, f32 = jnp.bfloat16, jnp.float32
    tile = pltpu.VMEM((g, m, c), bf)
    dma = pltpu.SemaphoreType.DMA
    hbm = pl.BlockSpec(memory_space=pl.ANY)
    vmem = pl.BlockSpec(memory_space=pltpu.VMEM)
    out = pl.pallas_call(
        functools.partial(body, ny, nx),
        out_shape=jax.ShapeDtypeStruct((rows, cols, c), bf),
        in_specs=[hbm, hbm, vmem, hbm, vmem],
        out_specs=hbm,
        scratch_shapes=[
            pltpu.VMEM((rows, cols, c), bf),
            pltpu.VMEM((g + 2, g + 2, D * D, c), bf),
            pltpu.VMEM((9, c, c), bf),
            pltpu.VMEM((9, c, c), bf),
            tile, tile, tile, tile, tile, tile, tile,
            pltpu.VMEM((g, m, c), f32),
            pltpu.VMEM((rows, cols, c), bf),
            dma((8,)), dma((8,)), dma((3,)),
            dma((2, g)), dma((2, g)), dma((2, g)), dma((2, g)), dma((g,)),
        ],
        compiler_params=pltpu.CompilerParams(
            collective_id=0, has_side_effects=True, vmem_limit_bytes=56 * 1024 * 1024),
        cost_estimate=pl.CostEstimate(
            flops=36 * rows * cols * c * c, bytes_accessed=16 * 2**20, transcendentals=0),
    )(inputs.reshape(rows, cols, c), nearby_kernel.reshape(9, c, c), nearby_bias,
      distant_kernel.reshape(9, c, c), distant_bias)
    return out.reshape(1, rows, cols, c)


def solution(mesh):
    placed = (P(None, "gy", "gx", None), P(), P(), P(), P())
    return jax.shard_map(
        on_device, mesh=mesh, in_specs=placed, out_specs=P(None, "gy", "gx", None), check_vma=False
    )
```
